32 devices in a mesh: ha: 8 (over y, x, core), wa: 4 (over z).
Axes of the slice: x: 2, y: 2, z: 4, core: 2. Of those that a mesh axis runs over, the one named last changes fastest.
Arguments:
- features: bfloat16 [1, 256, 256, 256], P(None, 'ha', 'wa'), may hold values from -6 to 6
- cotangent: bfloat16 [1, 256, 256, 256], P(None, 'ha', 'wa'), may hold values from -6 to 6
- qkv_weight: bfloat16 [256, 768], replicated, may hold values from -0.375 to 0.375
- out_weight: bfloat16 [256, 256], replicated, may hold values from -0.375 to 0.375
- up_weight: bfloat16 [256, 1024], replicated, may hold values from -0.375 to 0.375
- down_weight: bfloat16 [1024, 256], replicated, may hold values from -0.1875 to 0.1875
- norm_gains: float32 [2, 256], replicated, may hold values from 0.5 to 1.5
Outputs:
- grad_input: bfloat16 [1, 256, 256, 256], P(None, 'ha', 'wa')
- grad_qkv: float32 [256, 768], replicated
- grad_out: float32 [256, 256], replicated
- grad_up: float32 [256, 1024], replicated
- grad_down: float32 [1024, 256], replicated
- grad_gains: float32 [2, 256], replicated
The draws below stay inside these ranges and needn't reach their ends.
All inputs are finite; a program needn't handle non-finite values.
Results may differ from the reference program's by a relative error of at most 0.012.
Values may be sent and summed in bfloat16 or wider, within the bound.
A program may use at most 128 MiB of HBM per device.

```python
import math
import jax
import jax.numpy as jnp
from jax import lax

C = 256
HEADS = 8
GRID = 8
BATCH = 1
HIDDEN_SIZE = 1024
HEIGHT = 256
WIDTH = 256


def levels(key, shape, shards, low, largest):
    level, own = 1.0, jax.random.fold_in(key, 6)
    for position, shards_of in shards:
        draws = jnp.exp(jax.random.uniform(jax.random.fold_in(own, position), (shards_of,), jnp.float32, low / len(shards), largest / len(shards)))
        level = level * jnp.repeat(draws, shape[position] // shards_of).reshape([-1 if axis == position else 1 for axis in range(len(shape))])
    return level


def scatter_about(rng, dims, spread, bound, cuts=(), kind=jnp.bfloat16):
    factor_of = levels(rng, dims, cuts, -0.22, 0.18) if cuts else 1.0
    entries = jax.random.normal(rng, dims, jnp.float32) * spread * factor_of
    return jnp.minimum(jnp.maximum(entries, -bound), bound).astype(kind)


def setup_inputs(seed: int = 0) -> dict:
    seeds = jax.random.split(jax.random.key(seed), 8)
    return {
        "features": scatter_about(seeds[0], (BATCH, HEIGHT, WIDTH, C), 1.0, 6.0, ((1, 8), (2, 4))),
        "cotangent": scatter_about(seeds[1], (BATCH, HEIGHT, WIDTH, C), 1.0, 6.0, ((1, 8), (2, 4))),
        "qkv_weight": scatter_about(seeds[2], (C, 3 * C), C ** -0.5, 0.375),
        "out_weight": scatter_about(seeds[3], (C, C), C ** -0.5, 0.375),
        "up_weight": scatter_about(seeds[4], (C, HIDDEN_SIZE), C ** -0.5, 0.375),
        "down_weight": scatter_about(seeds[5], (HIDDEN_SIZE, C), HIDDEN_SIZE ** -0.5, 0.1875),
        "norm_gains": jnp.clip(1.0 + 0.1 * jax.random.normal(seeds[6], (2, C), jnp.float32), 0.5, 1.5),
    }


EPS = 1e-05

def norm_forward(rows, gain_row):
    values = rows.astype(jnp.float32)
    centre = values - lax.optimization_barrier(jnp.mean(values, axis=-1, keepdims=True))
    scaled = lax.rsqrt(lax.optimization_barrier(jnp.mean(centre * centre, axis=-1, keepdims=True)) + EPS)
    normed = centre * scaled
    return (normed, scaled, (normed * gain_row).astype(jnp.bfloat16))

def norm_backward(grad_rows, normed, scaled, gain_row):
    inner = grad_rows * gain_row
    first = lax.optimization_barrier(jnp.mean(inner, axis=-1, keepdims=True))
    second = lax.optimization_barrier(jnp.mean(inner * normed, axis=-1, keepdims=True))
    return (scaled * (inner - first - normed * second), lax.optimization_barrier(jnp.sum(grad_rows * normed, axis=0)))

def gelu_tanh(values):
    return jax.nn.gelu(values, approximate=True)

def attention_forward(qkv_grid):
    groups, members, triple = qkv_grid.shape
    head_dim = triple // (3 * HEADS)
    sections = qkv_grid.reshape(groups, members, 3, HEADS, head_dim).astype(jnp.float32)
    scores = jnp.einsum('gmhd,gnhd->ghmn', sections[:, :, 0], sections[:, :, 1]) * head_dim ** (-0.5)
    exp_scores = jnp.exp(scores)
    attend = exp_scores / lax.optimization_barrier(jnp.sum(exp_scores, axis=-1, keepdims=True))
    attend_low = attend.astype(jnp.bfloat16)
    context = jnp.einsum('ghmn,gnhd->gmhd', attend_low.astype(jnp.float32), sections[:, :, 2])
    return (context.astype(jnp.bfloat16).reshape(groups, members, HEADS * head_dim), attend, attend_low)

def attention_backward(qkv_grid, attend, attend_low, grad_grid):
    groups, members, triple = qkv_grid.shape
    head_dim = triple // (3 * HEADS)
    sections = qkv_grid.reshape(groups, members, 3, HEADS, head_dim).astype(jnp.float32)
    grad_heads = grad_grid.reshape(groups, members, HEADS, head_dim).astype(jnp.float32)
    grad_attend = jnp.einsum('gmhd,gnhd->ghmn', grad_heads, sections[:, :, 2])
    grad_value = jnp.einsum('ghmn,gmhd->gnhd', attend_low.astype(jnp.float32), grad_heads).astype(jnp.bfloat16)
    centred = grad_attend - lax.optimization_barrier(jnp.sum(attend * grad_attend, axis=-1, keepdims=True))
    grad_scores = (attend * centred * head_dim ** (-0.5)).astype(jnp.bfloat16).astype(jnp.float32)
    grad_query = jnp.einsum('ghmn,gnhd->gmhd', grad_scores, sections[:, :, 1]).astype(jnp.bfloat16)
    grad_key = jnp.einsum('ghmn,gmhd->gnhd', grad_scores, sections[:, :, 0]).astype(jnp.bfloat16)
    return jnp.stack([grad_query, grad_key, grad_value], axis=2).reshape(groups, members, triple)

def block_work(grouped_in, grouped_cot, qkv_weight, out_weight, up_weight, down_weight, norm_gains):
    groups, members, channels = grouped_in.shape
    flat_in = grouped_in.reshape(-1, channels)
    flat_cot = grouped_cot.reshape(-1, channels)
    normed_a, scaled_a, input_norm = norm_forward(flat_in, norm_gains[0])
    qkv_rows = jnp.dot(input_norm, qkv_weight, preferred_element_type=jnp.float32).astype(jnp.bfloat16)
    qkv_grid = qkv_rows.reshape(groups, members, 3 * channels)
    context_grid, attend, attend_low = attention_forward(qkv_grid)
    context = context_grid.reshape(-1, channels)
    hidden_res = (flat_in.astype(jnp.float32) + jnp.dot(context, out_weight, preferred_element_type=jnp.float32)).astype(jnp.bfloat16)
    normed_b, scaled_b, mid_norm = norm_forward(hidden_res, norm_gains[1])
    pre_act = jnp.dot(mid_norm, up_weight, preferred_element_type=jnp.float32)
    activated, gelu_back = jax.vjp(gelu_tanh, pre_act)
    act_low = activated.astype(jnp.bfloat16)
    grad_act = jnp.dot(flat_cot, down_weight.T, preferred_element_type=jnp.float32)
    grad_down = jnp.dot(act_low.T, flat_cot, preferred_element_type=jnp.float32)
    grad_pre = gelu_back(grad_act)[0].astype(jnp.bfloat16)
    grad_up = jnp.dot(mid_norm.T, grad_pre, preferred_element_type=jnp.float32)
    grad_mid = jnp.dot(grad_pre, up_weight.T, preferred_element_type=jnp.float32)
    res_grad, gain_b = norm_backward(grad_mid, normed_b, scaled_b, norm_gains[1])
    grad_hidden = (flat_cot.astype(jnp.float32) + res_grad).astype(jnp.bfloat16)
    grad_context = jnp.dot(grad_hidden, out_weight.T, preferred_element_type=jnp.float32).astype(jnp.bfloat16)
    grad_out = jnp.dot(context.T, grad_hidden, preferred_element_type=jnp.float32)
    grad_grid = attention_backward(qkv_grid, attend, attend_low, grad_context.reshape(groups, members, channels))
    grad_rows = grad_grid.reshape(-1, 3 * channels)
    grad_qkv = jnp.dot(input_norm.T, grad_rows, preferred_element_type=jnp.float32)
    grad_in_norm = jnp.dot(grad_rows, qkv_weight.T, preferred_element_type=jnp.float32)
    in_grad, gain_a = norm_backward(grad_in_norm, normed_a, scaled_a, norm_gains[0])
    grad_input = (grad_hidden.astype(jnp.float32) + in_grad).astype(jnp.bfloat16)
    sums = (grad_qkv, grad_out, grad_up, grad_down, jnp.stack([gain_a, gain_b]))
    return (sums, grad_input.reshape(groups, members, channels))

def reference(features, cotangent, qkv_weight, out_weight, up_weight, down_weight, norm_gains):
    members = GRID * GRID
    stride_h = HEIGHT // GRID
    stride_w = WIDTH // GRID
    count = BATCH * stride_h * stride_w
    per_block = math.gcd(count, 64)
    blocks = count // per_block

    def to_groups(full):
        arranged = full.reshape(BATCH, GRID, stride_h, GRID, stride_w, C)
        return jnp.transpose(arranged, (0, 2, 4, 1, 3, 5)).reshape(blocks, per_block, members, C)

    def step(carry, pair):
        sums, grad_block = block_work(pair[0], pair[1], qkv_weight, out_weight, up_weight, down_weight, norm_gains)
        return (tuple((held + new for held, new in zip(carry, sums))), grad_block)
    start = (jnp.zeros((C, 3 * C), jnp.float32), jnp.zeros((C, C), jnp.float32), jnp.zeros((C, HIDDEN_SIZE), jnp.float32), jnp.zeros((HIDDEN_SIZE, C), jnp.float32), jnp.zeros((2, C), jnp.float32))
    totals, grad_blocks = lax.scan(step, start, (to_groups(features), to_groups(cotangent)))
    arranged = grad_blocks.reshape(BATCH, stride_h, stride_w, GRID, GRID, C)
    grad_input = jnp.transpose(arranged, (0, 3, 1, 4, 2, 5)).reshape(BATCH, HEIGHT, WIDTH, C)
    root_count = float(BATCH * HEIGHT * WIDTH) ** 0.5
    return (grad_input, totals[0] / root_count, totals[1] / root_count, totals[2] / root_count, totals[3] / root_count, totals[4] / root_count)
```

```python
import functools
import math

import jax
import jax.numpy as jnp
from jax import lax
from jax.experimental import pallas as pl
from jax.experimental.pallas import tpu as pltpu
from jax.sharding import PartitionSpec as P

HEADS = 8
GRID = 8
EPS = 1e-05
LANES = 128
ROWS = 16
BF = jnp.bfloat16
F32 = jnp.float32


def mm(a, b, ca=1, cb=0):
    return lax.dot_general(a, b, (((ca,), (cb,)), ((), ())), preferred_element_type=F32)


def norm_forward(values, gain):
    centre = values - jnp.mean(values, axis=-1, keepdims=True)
    scaled = lax.rsqrt(jnp.mean(centre * centre, axis=-1, keepdims=True) + EPS)
    return centre * scaled, scaled


def norm_backward(grad, normed, scaled, gain):
    inner = grad * gain
    first = jnp.mean(inner, axis=-1, keepdims=True)
    second = jnp.mean(inner * normed, axis=-1, keepdims=True)
    return scaled * (inner - first - normed * second)


def head_masks(members, head_dim):
    lane = lax.broadcasted_iota(jnp.int32, (members, LANES), 1) // head_dim
    return [lane == h for h in range(LANES // head_dim)]


def spread(part, masks):
    zero = jnp.zeros_like(part)
    return jnp.concatenate([jnp.where(m, part, zero) for m in masks], axis=0)


def collect(blocks, masks, members):
    out = blocks[:members]
    for h in range(1, len(masks)):
        out = jnp.where(masks[h], blocks[h * members : (h + 1) * members], out)
    return out


def chunk_work(
    load_in, load_cot, store_out, first,
    wqkv, wout, wup, wdown, gains,
    a_qkv, a_out, a_up, a_down, a_gains,
    reg, qkv, probs, mid, rows_out,
):
    rows, channels = mid.shape
    members = GRID * GRID
    head_dim = channels // HEADS
    groups = rows // members
    halves = channels // LANES
    scale = head_dim ** (-0.5)
    masks = head_masks(members, head_dim)
    per_half = len(masks)
    wide = per_half * members

    def add_to(ref, index, value):
        ref[index] = ref[index] + value

    def grouped(load):
        flat = load().astype(F32)
        for half in range(halves):
            reg[half] = flat[:, half * LANES : (half + 1) * LANES]
        return jnp.concatenate(
            [
                jnp.concatenate(
                    [reg[half, pl.ds(j, members, stride=groups), :] for half in range(halves)],
                    axis=1,
                )
                for j in range(groups)
            ],
            axis=0,
        )

    gain_a, gain_b = gains[0:1, :], gains[1:2, :]
    cot = grouped(load_cot)
    cot_low = cot.astype(BF)
    values = grouped(load_in)
    normed_a, scaled_a = norm_forward(values, gain_a)
    input_norm = (normed_a * gain_a).astype(BF)
    qkv[...] = mm(input_norm, wqkv[...]).astype(BF)

    def section(g, which, half):
        start = which * channels + half * LANES
        return qkv[g * members : (g + 1) * members, start : start + LANES]

    for g in range(groups):
        for half in range(halves):
            q, k, v = (section(g, which, half) for which in range(3))
            e = jnp.exp(mm(k, spread(q, masks), 1, 1) * scale)
            p = e / jnp.sum(e, axis=0, keepdims=True)
            probs[g, half] = p
            ctx = collect(mm(p.astype(BF), v, 0, 0), masks, members)
            mid[g * members : (g + 1) * members, half * LANES : (half + 1) * LANES] = ctx.astype(BF)

    context = mid[...]
    hidden = (values + mm(context, wout[...])).astype(BF).astype(F32)
    normed_b, scaled_b = norm_forward(hidden, gain_b)
    mid_norm = (normed_b * gain_b).astype(BF)
    root = math.sqrt(2.0 / math.pi)
    grad_mid = None
    width = 256
    for start in range(0, wup.shape[1], width):
        cols = slice(start, start + width)
        pre = mm(mid_norm, wup[:, cols])
        square = pre * pre
        t = jnp.tanh(root * (pre + 0.044715 * (square * pre)))
        half_up = 0.5 * (1.0 + t)
        act = (pre * half_up).astype(BF)
        slope = half_up + (0.5 * root) * pre * (1.0 - t * t) * (1.0 + (3 * 0.044715) * square)
        grad_pre = (mm(cot_low, wdown[cols, :], 1, 1) * slope).astype(BF)
        add_to(a_down, (slice(None), cols), mm(cot_low, act, 0, 0))
        add_to(a_up, (slice(None), cols), mm(mid_norm, grad_pre, 0, 0))
        part = mm(grad_pre, wup[:, cols], 1, 1)
        grad_mid = part if grad_mid is None else grad_mid + part
    add_to(a_gains, (slice(1, 2), slice(None)), jnp.sum(grad_mid * normed_b, axis=0, keepdims=True))
    grad_hidden = (cot + norm_backward(grad_mid, normed_b, scaled_b, gain_b)).astype(BF)
    add_to(a_out, Ellipsis, mm(context, grad_hidden, 0, 0))
    mid[...] = mm(grad_hidden, wout[...], 1, 1).astype(BF)

    for g in range(groups):
        at = slice(g * members, (g + 1) * members)
        for half in range(halves):
            q, k, v = (section(g, which, half) for which in range(3))
            p = probs[g, half]
            gc = spread(mid[at, half * LANES : (half + 1) * LANES], masks)
            gp = mm(v, gc, 1, 1)
            gs = (p * (gp - jnp.sum(p * gp, axis=0, keepdims=True)) * scale).astype(BF)
            grads = (
                collect(mm(gs, k, 0, 0), masks, members),
                mm(gs, spread(q, masks)),
                mm(p.astype(BF), gc),
            )
            for which in range(3):
                begin = which * channels + half * LANES
                rows_out[at, begin : begin + LANES] = grads[which].astype(BF)

    grad_rows = rows_out[...]
    add_to(a_qkv, Ellipsis, mm(input_norm, grad_rows, 0, 0))
    grad_norm = mm(grad_rows, wqkv[...], 1, 1)
    add_to(a_gains, (slice(0, 1), slice(None)), jnp.sum(grad_norm * normed_a, axis=0, keepdims=True))
    result = grad_hidden.astype(F32) + norm_backward(grad_norm, normed_a, scaled_a, gain_a)
    for half in range(halves):
        for j in range(groups):
            reg[half, pl.ds(j, members, stride=groups), :] = result[
                j * members : (j + 1) * members, half * LANES : (half + 1) * LANES
            ]
    store_out(jnp.concatenate([reg[half] for half in range(halves)], axis=1).astype(BF))


def local_kernel(x_ref, wqkv, wout, wup, wdown, gains, o_ref, *rest):
    sums, scratch = rest[:5], rest[5:]
    peers, _, _, piece, channels = x_ref.shape
    rows = peers * piece

    @pl.when(pl.program_id(0) == 0)
    def _():
        for ref in sums:
            ref[...] = jnp.zeros_like(ref)

    def store(value):
        o_ref[:, 0] = value.reshape(peers, piece, channels)

    chunk_work(
        lambda: x_ref[:, 0, 0].reshape(rows, channels),
        lambda: x_ref[:, 0, 1].reshape(rows, channels),
        store, None, wqkv, wout, wup, wdown, gains, *sums, *scratch,
    )


def scratch_of(rows, channels):
    members = GRID * GRID
    halves = channels // LANES
    wide = (HEADS // halves) * members
    return [
        pltpu.VMEM((halves, rows, LANES), F32),
        pltpu.VMEM((rows, 3 * channels), BF),
        pltpu.VMEM((rows // members, halves, members, wide), F32),
        pltpu.VMEM((rows, channels), BF),
        pltpu.VMEM((rows, 3 * channels), BF),
    ]


def local_call(x, wqkv, wout, wup, wdown, gains):
    peers, chunks, _, piece, channels = x.shape
    hidden = wup.shape[1]

    def whole(shape):
        return pl.BlockSpec(shape, lambda c: (0,) * len(shape))

    sums = [(channels, 3 * channels), (channels, channels), (channels, hidden), (channels, hidden), (2, channels)]
    return pl.pallas_call(
        local_kernel,
        grid=(chunks,),
        in_specs=[pl.BlockSpec((peers, 1, 2, piece, channels), lambda c: (0, c, 0, 0, 0))]
        + [whole(a.shape) for a in (wqkv, wout, wup, wdown, gains)],
        out_specs=[pl.BlockSpec((peers, 1, piece, channels), lambda c: (0, c, 0, 0))]
        + [whole(s) for s in sums],
        out_shape=[jax.ShapeDtypeStruct((peers, chunks, piece, channels), BF)]
        + [jax.ShapeDtypeStruct(s, F32) for s in sums],
        scratch_shapes=scratch_of(peers * piece, channels),
        compiler_params=pltpu.CompilerParams(vmem_limit_bytes=56 << 20),
    )(x, wqkv, wout, wup, wdown, gains)


def layout(rows_dev, cols_dev, tile_rows, tile_cols):
    stride_h = tile_rows * rows_dev // GRID
    stride_w = tile_cols * cols_dev // GRID
    classes = max(1, stride_h // tile_rows)
    assert stride_h == classes * tile_rows and tile_cols % stride_w == 0
    inner = tile_cols // stride_w
    peers = rows_dev // classes * cols_dev
    mine = tile_rows * stride_w // peers
    assert tile_rows * stride_w == mine * peers and stride_w % mine == 0
    per_chunk = ROWS // inner
    assert mine % per_chunk == 0
    return classes, inner, peers, stride_w // mine, mine // per_chunk, per_chunk


def shards(mesh_shape, features, cotangent, qkv_weight, out_weight, up_weight, down_weight, norm_gains):
    images, tile_rows, tile_cols, channels = features.shape
    rows_dev, cols_dev = mesh_shape["ha"], mesh_shape["wa"]
    classes, inner, peers, cuts, chunks, per_chunk = layout(rows_dev, cols_dev, tile_rows, tile_cols)
    split = (tile_rows, inner, cuts, chunks, per_chunk, channels)

    def pack(tile):
        cut = jnp.transpose(tile.reshape(split), (0, 2, 3, 1, 4, 5))
        return cut.reshape(peers, chunks, ROWS, channels)

    def unpack(packed):
        cut = packed.reshape(tile_rows, cuts, chunks, inner, per_chunk, channels)
        return jnp.transpose(cut, (0, 3, 1, 2, 4, 5)).reshape(images, tile_rows, tile_cols, channels)

    def exchange(x):
        if classes == 1:
            return lax.all_to_all(x, ("ha", "wa"), 0, 0, tiled=True)
        everyone = [
            [(h * classes + c) * cols_dev + w for h in range(rows_dev // classes) for w in range(cols_dev)]
            for c in range(classes)
        ]
        return lax.all_to_all(x, ("ha", "wa"), 0, 0, tiled=True, axis_index_groups=everyone)

    arrived = exchange(jnp.stack([pack(features), pack(cotangent)], axis=2))
    done, *sums = local_call(arrived, qkv_weight, out_weight, up_weight, down_weight, norm_gains)
    totals = lax.psum(tuple(sums), ("ha", "wa"))
    grad_input = unpack(exchange(done))
    factor = 1.0 / float(images * tile_rows * tile_cols * rows_dev * cols_dev) ** 0.5
    return (
        grad_input,
        totals[0] * factor,
        totals[1] * factor,
        totals[2] * factor,
        totals[3].T * factor,
        totals[4] * factor,
    )


def solution(mesh):
    return jax.shard_map(
        functools.partial(shards, dict(mesh.shape)),
        mesh=mesh,
        in_specs=(P(None, "ha", "wa", None), P(None, "ha", "wa", None), P(), P(), P(), P(), P()),
        out_specs=(P(None, "ha", "wa", None), P(), P(), P(), P(), P()),
        check_vma=False,
    )
```

```python
import functools
import math

import jax
import jax.numpy as jnp
from jax import lax
from jax.experimental import pallas as pl
from jax.experimental.pallas import tpu as pltpu
from jax.sharding import PartitionSpec as P

HEADS = 8
GRID = 8
EPS = 1e-05
LANES = 128
ROWS = 16
BF = jnp.bfloat16
F32 = jnp.float32


def mm(a, b, ca=1, cb=0):
    return lax.dot_general(a, b, (((ca,), (cb,)), ((), ())), preferred_element_type=F32)


def norm_forward(values, gain):
    centre = values - jnp.mean(values, axis=-1, keepdims=True)
    scaled = lax.rsqrt(jnp.mean(centre * centre, axis=-1, keepdims=True) + EPS)
    return centre * scaled, scaled


def norm_backward(grad, normed, scaled, gain):
    inner = grad * gain
    first = jnp.mean(inner, axis=-1, keepdims=True)
    second = jnp.mean(inner * normed, axis=-1, keepdims=True)
    return scaled * (inner - first - normed * second)


def head_masks(members, head_dim):
    lane = lax.broadcasted_iota(jnp.int32, (members, LANES), 1) // head_dim
    return [lane == h for h in range(LANES // head_dim)]


def spread(part, masks):
    zero = jnp.zeros_like(part)
    return jnp.concatenate([jnp.where(m, part, zero) for m in masks], axis=0)


def collect(blocks, masks, members):
    out = blocks[:members]
    for h in range(1, len(masks)):
        out = jnp.where(masks[h], blocks[h * members : (h + 1) * members], out)
    return out


def chunk_work(
    load_in, load_cot, store_out, first,
    wqkv, wout, wup, wdown, gains,
    a_qkv, a_out, a_up, a_down, a_gains,
    reg, qkv, probs, mid, rows_out,
):
    rows, channels = mid.shape
    members = GRID * GRID
    head_dim = channels // HEADS
    groups = rows // members
    halves = channels // LANES
    scale = head_dim ** (-0.5)
    masks = head_masks(members, head_dim)
    per_half = len(masks)
    wide = per_half * members

    def add_to(ref, index, value):
        ref[index] = ref[index] + value

    def grouped(load):
        flat = load().astype(F32)
        for half in range(halves):
            reg[half] = flat[:, half * LANES : (half + 1) * LANES]
        return jnp.concatenate(
            [
                jnp.concatenate(
                    [reg[half, pl.ds(j, members, stride=groups), :] for half in range(halves)],
                    axis=1,
                )
                for j in range(groups)
            ],
            axis=0,
        )

    gain_a, gain_b = gains[0:1, :], gains[1:2, :]
    cot = grouped(load_cot)
    cot_low = cot.astype(BF)
    values = grouped(load_in)
    normed_a, scaled_a = norm_forward(values, gain_a)
    input_norm = (normed_a * gain_a).astype(BF)
    qkv[...] = mm(input_norm, wqkv[...]).astype(BF)

    def section(g, which, half):
        start = which * channels + half * LANES
        return qkv[g * members : (g + 1) * members, start : start + LANES]

    for g in range(groups):
        for half in range(halves):
            q, k, v = (section(g, which, half) for which in range(3))
            e = jnp.exp(mm(k, spread(q, masks), 1, 1) * scale)
            p = e / jnp.sum(e, axis=0, keepdims=True)
            probs[g, half] = p
            ctx = collect(mm(p.astype(BF), v, 0, 0), masks, members)
            mid[g * members : (g + 1) * members, half * LANES : (half + 1) * LANES] = ctx.astype(BF)

    context = mid[...]
    hidden = (values + mm(context, wout[...])).astype(BF).astype(F32)
    normed_b, scaled_b = norm_forward(hidden, gain_b)
    mid_norm = (normed_b * gain_b).astype(BF)
    root = math.sqrt(2.0 / math.pi)
    grad_mid = None
    width = 256
    for start in range(0, wup.shape[1], width):
        cols = slice(start, start + width)
        pre = mm(mid_norm, wup[:, cols])
        square = pre * pre
        t = jnp.tanh(root * (pre + 0.044715 * (square * pre)))
        half_up = 0.5 * (1.0 + t)
        act = (pre * half_up).astype(BF)
        slope = half_up + (0.5 * root) * pre * (1.0 - t * t) * (1.0 + (3 * 0.044715) * square)
        grad_pre = (mm(cot_low, wdown[cols, :], 1, 1) * slope).astype(BF)
        add_to(a_down, (slice(None), cols), mm(cot_low, act, 0, 0))
        add_to(a_up, (slice(None), cols), mm(mid_norm, grad_pre, 0, 0))
        part = mm(grad_pre, wup[:, cols], 1, 1)
        grad_mid = part if grad_mid is None else grad_mid + part
    add_to(a_gains, (slice(1, 2), slice(None)), jnp.sum(grad_mid * normed_b, axis=0, keepdims=True))
    grad_hidden = (cot + norm_backward(grad_mid, normed_b, scaled_b, gain_b)).astype(BF)
    add_to(a_out, Ellipsis, mm(context, grad_hidden, 0, 0))
    mid[...] = mm(grad_hidden, wout[...], 1, 1).astype(BF)

    for g in range(groups):
        at = slice(g * members, (g + 1) * members)
        for half in range(halves):
            q, k, v = (section(g, which, half) for which in range(3))
            p = probs[g, half]
            gc = spread(mid[at, half * LANES : (half + 1) * LANES], masks)
            gp = mm(v, gc, 1, 1)
            gs = (p * (gp - jnp.sum(p * gp, axis=0, keepdims=True)) * scale).astype(BF)
            grads = (
                collect(mm(gs, k, 0, 0), masks, members),
                mm(gs, spread(q, masks)),
                mm(p.astype(BF), gc),
            )
            for which in range(3):
                begin = which * channels + half * LANES
                rows_out[at, begin : begin + LANES] = grads[which].astype(BF)

    grad_rows = rows_out[...]
    add_to(a_qkv, Ellipsis, mm(input_norm, grad_rows, 0, 0))
    grad_norm = mm(grad_rows, wqkv[...], 1, 1)
    add_to(a_gains, (slice(0, 1), slice(None)), jnp.sum(grad_norm * normed_a, axis=0, keepdims=True))
    result = grad_hidden.astype(F32) + norm_backward(grad_norm, normed_a, scaled_a, gain_a)
    for half in range(halves):
        for j in range(groups):
            reg[half, pl.ds(j, members, stride=groups), :] = result[
                j * members : (j + 1) * members, half * LANES : (half + 1) * LANES
            ]
    store_out(jnp.concatenate([reg[half] for half in range(halves)], axis=1).astype(BF))


def local_kernel(x_ref, wqkv, wout, wup, wdown, gains, o_ref, *rest):
    sums, scratch = rest[:5], rest[5:]
    peers, _, _, piece, channels = x_ref.shape
    rows = peers * piece

    @pl.when(pl.program_id(0) == 0)
    def _():
        for ref in sums:
            ref[...] = jnp.zeros_like(ref)

    def store(value):
        o_ref[:, 0] = value.reshape(peers, piece, channels)

    chunk_work(
        lambda: x_ref[:, 0, 0].reshape(rows, channels),
        lambda: x_ref[:, 0, 1].reshape(rows, channels),
        store, None, wqkv, wout, wup, wdown, gains, *sums, *scratch,
    )


def scratch_of(rows, channels):
    members = GRID * GRID
    halves = channels // LANES
    wide = (HEADS // halves) * members
    return [
        pltpu.VMEM((halves, rows, LANES), F32),
        pltpu.VMEM((rows, 3 * channels), BF),
        pltpu.VMEM((rows // members, halves, members, wide), F32),
        pltpu.VMEM((rows, channels), BF),
        pltpu.VMEM((rows, 3 * channels), BF),
    ]


def local_call(x, wqkv, wout, wup, wdown, gains):
    peers, chunks, _, piece, channels = x.shape
    hidden = wup.shape[1]

    def whole(shape):
        return pl.BlockSpec(shape, lambda c: (0,) * len(shape))

    sums = [(channels, 3 * channels), (channels, channels), (channels, hidden), (channels, hidden), (2, channels)]
    return pl.pallas_call(
        local_kernel,
        grid=(chunks,),
        in_specs=[pl.BlockSpec((peers, 1, 2, piece, channels), lambda c: (0, c, 0, 0, 0))]
        + [whole(a.shape) for a in (wqkv, wout, wup, wdown, gains)],
        out_specs=[pl.BlockSpec((peers, 1, piece, channels), lambda c: (0, c, 0, 0))]
        + [whole(s) for s in sums],
        out_shape=[jax.ShapeDtypeStruct((peers, chunks, piece, channels), BF)]
        + [jax.ShapeDtypeStruct(s, F32) for s in sums],
        scratch_shapes=scratch_of(peers * piece, channels),
        compiler_params=pltpu.CompilerParams(vmem_limit_bytes=56 << 20),
    )(x, wqkv, wout, wup, wdown, gains)


def reduce_kernel(
    rows_dev, cols_dev, factor,
    s_qkv, s_out, s_up, s_down, s_gain,
    o_qkv, o_out, o_up, o_down, o_gain,
    work, send, recv, total, gsend, grecv, gwide, send_sem, recv_sem,
):
    mesh_id = pl.DeviceIdType.MESH
    bits = rows_dev.bit_length() - 1
    half_rows = work.shape[1]
    ha, wa = lax.axis_index("ha"), lax.axis_index("wa")
    side = [(ha // (1 << b)) % 2 for b in range(bits)]
    partner = [(ha + (1 - 2 * side[b]) * (1 << b), wa) for b in range(bits)]
    across = [(ha, lax.rem(wa + i, cols_dev)) for i in range(1, cols_dev)]

    barrier = pltpu.get_barrier_semaphore()
    for device in partner + across:
        pl.semaphore_signal(barrier, inc=1, device_id=device, device_id_type=mesh_id)
    pl.semaphore_wait(barrier, len(partner) + len(across))

    count = [0]
    copies = []

    def push(src, dst, device):
        k = count[0]
        count[0] += 1
        copy = pltpu.make_async_remote_copy(
            src_ref=src, dst_ref=dst, send_sem=send_sem.at[k], recv_sem=recv_sem.at[k],
            device_id=device, device_id_type=mesh_id,
        )
        copy.start()
        copies.append(copy)
        return copy

    places = []
    block = s_qkv.shape[0]
    per_half = half_rows // block
    for src, dst, flip in ((s_qkv, o_qkv, 0), (s_out, o_out, 0), (s_up, o_up, 0), (s_down, o_down, 1)):
        for start in range(0, src.shape[1], LANES):
            places.append((src, dst, flip, start))
    used = -(-len(places) // 2)
    for n, (src, _, _, start) in enumerate(places):
        row = n % used * block
        work[n // used, row : row + block, :] = src[:, start : start + LANES]
    if used < per_half:
        work[:, used * block :, :] = jnp.zeros((2, half_rows - used * block, LANES), F32)

    def span(start, size):
        return pl.ds(pl.multiple_of(start, ROWS), size)

    orders = [[0] + list(range(1, bits)), [0] + list(range(bits - 1, 0, -1))]
    start = [0, 0]
    size = half_rows
    offset = 0
    pending = [None, None]
    gsend[0] = jnp.zeros(gsend.shape[1:], F32)
    gsend[0, 0:2, :] = s_gain[...]
    gpending = None

    def absorb(h):
        if pending[h] is None:
            return
        copy, at, n = pending[h]
        copy.wait_recv()
        place = span(start[h], n)
        work[h, place, :] = work[h, place, :] + recv[h, at : at + n, :].astype(F32)

    for step in range(bits):
        half = size // 2
        for h in range(2):
            absorb(h)
            b = orders[h][step]
            send[h, offset : offset + half, :] = work[h, span(start[h] + (1 - side[b]) * half, half), :].astype(BF)
            copy = push(
                send.at[h, pl.ds(offset, half), :], recv.at[h, pl.ds(offset, half), :], partner[b]
            )
            start[h] = start[h] + side[b] * half
            pending[h] = (copy, offset, half)
        if step > 0:
            gpending.wait_recv()
            gsend[step] = gsend[step - 1] + grecv[step - 1]
        gpending = push(gsend.at[step], grecv.at[step], partner[step])
        offset += half
        size = half

    shard = size // cols_dev
    arrivals = [[], []]
    for h in range(2):
        absorb(h)
        for i in range(1, cols_dev):
            peer = across[i - 1]
            at = offset + (i - 1) * shard
            send[h, at : at + shard, :] = work[h, span(start[h] + peer[1] * shard, shard), :].astype(BF)
            arrivals[h].append(
                push(send.at[h, pl.ds(at, shard), :], recv.at[h, pl.ds(at, shard), :], peer)
            )
    gpending.wait_recv()
    gwide[wa] = gsend[bits - 1] + grecv[bits - 1]
    garrivals = [push(gwide.at[wa], gwide.at[wa], peer) for peer in across]

    gathers = [[], []]
    for h in range(2):
        mine = span(start[h] + wa * shard, shard)
        value = work[h, mine, :]
        for i in range(1, cols_dev):
            arrivals[h][i - 1].wait_recv()
            at = offset + (i - 1) * shard
            value = value + recv[h, at : at + shard, :].astype(F32)
        total[h, mine, :] = value.astype(BF)
        for peer in across:
            gathers[h].append(push(total.at[h, mine, :], total.at[h, mine, :], peer))
    for step in reversed(range(bits)):
        for h in range(2):
            for copy in gathers[h]:
                copy.wait_recv()
            b = orders[h][step]
            held = total.at[h, span(start[h], size), :]
            gathers[h] = [push(held, held, partner[b])]
            start[h] = start[h] - side[b] * size
        size = size * 2
    for copy in garrivals:
        copy.wait_recv()
    gain = gwide[0]
    for i in range(1, cols_dev):
        gain = gain + gwide[i]
    o_gain[...] = gain[0:2, :] * factor
    for h in range(2):
        for copy in gathers[h]:
            copy.wait_recv()
    for n, (_, dst, flip, at) in enumerate(places):
        row = n % used * block
        value = total[n // used, row : row + block, :].astype(F32) * factor
        if flip:
            dst[at : at + LANES, :] = value.T
        else:
            dst[:, at : at + LANES] = value
    for copy in copies:
        copy.wait_send()


def reduce_scratch(rows_dev, cols_dev, elements, channels):
    bits = rows_dev.bit_length() - 1
    unit = ROWS * rows_dev * cols_dev
    half_rows = -(-elements // (2 * LANES * unit)) * unit
    moved = half_rows - half_rows // rows_dev + half_rows // rows_dev // cols_dev * (cols_dev - 1)
    number = 5 * (cols_dev - 1) + 5 * bits
    return [
        pltpu.VMEM((2, half_rows, LANES), F32),
        pltpu.VMEM((2, moved, LANES), BF),
        pltpu.VMEM((2, moved, LANES), BF),
        pltpu.VMEM((2, half_rows, LANES), BF),
        pltpu.VMEM((bits, 8, channels), F32),
        pltpu.VMEM((bits, 8, channels), F32),
        pltpu.VMEM((cols_dev, 8, channels), F32),
        pltpu.SemaphoreType.DMA((number,)),
        pltpu.SemaphoreType.DMA((number,)),
    ]


def reduce_call(rows_dev, cols_dev, factor, sums):
    shapes = [s.shape for s in sums]
    shapes[3] = shapes[3][::-1]
    elements = sum(math.prod(s) for s in shapes[:4])
    return pl.pallas_call(
        functools.partial(reduce_kernel, rows_dev, cols_dev, factor),
        in_specs=[pl.BlockSpec(memory_space=pltpu.VMEM)] * 5,
        out_specs=[pl.BlockSpec(memory_space=pltpu.VMEM)] * 5,
        out_shape=[jax.ShapeDtypeStruct(s, F32) for s in shapes],
        scratch_shapes=reduce_scratch(rows_dev, cols_dev, elements, shapes[0][0]),
        compiler_params=pltpu.CompilerParams(
            collective_id=0, has_side_effects=True, vmem_limit_bytes=40 << 20
        ),
    )(*sums)


def layout(rows_dev, cols_dev, tile_rows, tile_cols):
    stride_h = tile_rows * rows_dev // GRID
    stride_w = tile_cols * cols_dev // GRID
    classes = max(1, stride_h // tile_rows)
    assert stride_h == classes * tile_rows and tile_cols % stride_w == 0
    inner = tile_cols // stride_w
    peers = rows_dev // classes * cols_dev
    mine = tile_rows * stride_w // peers
    assert tile_rows * stride_w == mine * peers and stride_w % mine == 0
    per_chunk = ROWS // inner
    assert mine % per_chunk == 0
    return classes, inner, peers, stride_w // mine, mine // per_chunk, per_chunk


def shards(mesh_shape, features, cotangent, qkv_weight, out_weight, up_weight, down_weight, norm_gains):
    images, tile_rows, tile_cols, channels = features.shape
    rows_dev, cols_dev = mesh_shape["ha"], mesh_shape["wa"]
    classes, inner, peers, cuts, chunks, per_chunk = layout(rows_dev, cols_dev, tile_rows, tile_cols)
    split = (tile_rows, inner, cuts, chunks, per_chunk, channels)

    def pack(tile):
        cut = jnp.transpose(tile.reshape(split), (0, 2, 3, 1, 4, 5))
        return cut.reshape(peers, chunks, ROWS, channels)

    def unpack(packed):
        cut = packed.reshape(tile_rows, cuts, chunks, inner, per_chunk, channels)
        return jnp.transpose(cut, (0, 3, 1, 2, 4, 5)).reshape(images, tile_rows, tile_cols, channels)

    def exchange(x):
        if classes == 1:
            return lax.all_to_all(x, ("ha", "wa"), 0, 0, tiled=True)
        everyone = [
            [(h * classes + c) * cols_dev + w for h in range(rows_dev // classes) for w in range(cols_dev)]
            for c in range(classes)
        ]
        return lax.all_to_all(x, ("ha", "wa"), 0, 0, tiled=True, axis_index_groups=everyone)

    arrived = exchange(jnp.stack([pack(features), pack(cotangent)], axis=2))
    done, *sums = local_call(arrived, qkv_weight, out_weight, up_weight, down_weight, norm_gains)
    factor = 1.0 / float(images * tile_rows * tile_cols * rows_dev * cols_dev) ** 0.5
    totals = reduce_call(rows_dev, cols_dev, factor, sums)
    return (unpack(exchange(done)), *totals)


def solution(mesh):
    return jax.shard_map(
        functools.partial(shards, dict(mesh.shape)),
        mesh=mesh,
        in_specs=(P(None, "ha", "wa", None), P(None, "ha", "wa", None), P(), P(), P(), P(), P()),
        out_specs=(P(None, "ha", "wa", None), P(), P(), P(), P(), P()),
        check_vma=False,
    )
```

```python
import functools
import math

import jax
import jax.numpy as jnp
from jax import lax
from jax.experimental import pallas as pl
from jax.experimental.pallas import tpu as pltpu
from jax.sharding import PartitionSpec as P

HEADS = 8
GRID = 8
EPS = 1e-05
LANES = 128
ROWS = 16
BF = jnp.bfloat16
F32 = jnp.float32


def mm(a, b, ca=1, cb=0):
    return lax.dot_general(a, b, (((ca,), (cb,)), ((), ())), preferred_element_type=F32)


def norm_forward(values, gain):
    centre = values - jnp.mean(values, axis=-1, keepdims=True)
    scaled = lax.rsqrt(jnp.mean(centre * centre, axis=-1, keepdims=True) + EPS)
    return centre * scaled, scaled


def norm_backward(grad, normed, scaled, gain):
    inner = grad * gain
    first = jnp.mean(inner, axis=-1, keepdims=True)
    second = jnp.mean(inner * normed, axis=-1, keepdims=True)
    return scaled * (inner - first - normed * second)


def head_masks(members, head_dim):
    lane = lax.broadcasted_iota(jnp.int32, (members, LANES), 1) // head_dim
    return [lane == h for h in range(LANES // head_dim)]


def spread(part, masks):
    zero = jnp.zeros_like(part)
    return jnp.concatenate([jnp.where(m, part, zero) for m in masks], axis=0)


def collect(blocks, masks, members):
    out = blocks[:members]
    for h in range(1, len(masks)):
        out = jnp.where(masks[h], blocks[h * members : (h + 1) * members], out)
    return out


def chunk_work(
    load_in, load_cot, store_out, first,
    wqkv, wout, wup, wdown, gains,
    a_qkv, a_out, a_up, a_down, a_gains,
    reg, qkv, probs, mid, rows_out,
):
    rows, channels = mid.shape
    members = GRID * GRID
    head_dim = channels // HEADS
    groups = rows // members
    halves = channels // LANES
    scale = head_dim ** (-0.5)
    masks = head_masks(members, head_dim)
    per_half = len(masks)
    wide = per_half * members

    def add_to(ref, index, value):
        ref[index] = ref[index] + value

    def grouped(load):
        flat = load().astype(F32)
        for half in range(halves):
            reg[half] = flat[:, half * LANES : (half + 1) * LANES]
        return jnp.concatenate(
            [
                jnp.concatenate(
                    [reg[half, pl.ds(j, members, stride=groups), :] for half in range(halves)],
                    axis=1,
                )
                for j in range(groups)
            ],
            axis=0,
        )

    gain_a, gain_b = gains[0:1, :], gains[1:2, :]
    cot = grouped(load_cot)
    cot_low = cot.astype(BF)
    values = grouped(load_in)
    normed_a, scaled_a = norm_forward(values, gain_a)
    input_norm = (normed_a * gain_a).astype(BF)
    qkv[...] = mm(input_norm, wqkv[...]).astype(BF)

    def section(g, which, half):
        start = which * channels + half * LANES
        return qkv[g * members : (g + 1) * members, start : start + LANES]

    for g in range(groups):
        for half in range(halves):
            q, k, v = (section(g, which, half) for which in range(3))
            e = jnp.exp(mm(k, spread(q, masks), 1, 1) * scale)
            p = e / jnp.sum(e, axis=0, keepdims=True)
            probs[g, half] = p
            ctx = collect(mm(p.astype(BF), v, 0, 0), masks, members)
            mid[g * members : (g + 1) * members, half * LANES : (half + 1) * LANES] = ctx.astype(BF)

    context = mid[...]
    hidden = (values + mm(context, wout[...])).astype(BF).astype(F32)
    normed_b, scaled_b = norm_forward(hidden, gain_b)
    mid_norm = (normed_b * gain_b).astype(BF)
    root = math.sqrt(2.0 / math.pi)
    grad_mid = None
    width = 256
    for start in range(0, wup.shape[1], width):
        cols = slice(start, start + width)
        pre = mm(mid_norm, wup[:, cols])
        square = pre * pre
        t = jnp.tanh(root * (pre + 0.044715 * (square * pre)))
        half_up = 0.5 * (1.0 + t)
        act = (pre * half_up).astype(BF)
        slope = half_up + (0.5 * root) * pre * (1.0 - t * t) * (1.0 + (3 * 0.044715) * square)
        grad_pre = (mm(cot_low, wdown[cols, :], 1, 1) * slope).astype(BF)
        add_to(a_down, (slice(None), cols), mm(cot_low, act, 0, 0))
        add_to(a_up, (slice(None), cols), mm(mid_norm, grad_pre, 0, 0))
        part = mm(grad_pre, wup[:, cols], 1, 1)
        grad_mid = part if grad_mid is None else grad_mid + part
    add_to(a_gains, (slice(1, 2), slice(None)), jnp.sum(grad_mid * normed_b, axis=0, keepdims=True))
    grad_hidden = (cot + norm_backward(grad_mid, normed_b, scaled_b, gain_b)).astype(BF)
    add_to(a_out, Ellipsis, mm(context, grad_hidden, 0, 0))
    mid[...] = mm(grad_hidden, wout[...], 1, 1).astype(BF)

    for g in range(groups):
        at = slice(g * members, (g + 1) * members)
        for half in range(halves):
            q, k, v = (section(g, which, half) for which in range(3))
            p = probs[g, half]
            gc = spread(mid[at, half * LANES : (half + 1) * LANES], masks)
            gp = mm(v, gc, 1, 1)
            gs = (p * (gp - jnp.sum(p * gp, axis=0, keepdims=True)) * scale).astype(BF)
            grads = (
                collect(mm(gs, k, 0, 0), masks, members),
                mm(gs, spread(q, masks)),
                mm(p.astype(BF), gc),
            )
            for which in range(3):
                begin = which * channels + half * LANES
                rows_out[at, begin : begin + LANES] = grads[which].astype(BF)

    grad_rows = rows_out[...]
    add_to(a_qkv, Ellipsis, mm(input_norm, grad_rows, 0, 0))
    grad_norm = mm(grad_rows, wqkv[...], 1, 1)
    add_to(a_gains, (slice(0, 1), slice(None)), jnp.sum(grad_norm * normed_a, axis=0, keepdims=True))
    result = grad_hidden.astype(F32) + norm_backward(grad_norm, normed_a, scaled_a, gain_a)
    for half in range(halves):
        for j in range(groups):
            reg[half, pl.ds(j, members, stride=groups), :] = result[
                j * members : (j + 1) * members, half * LANES : (half + 1) * LANES
            ]
    store_out(jnp.concatenate([reg[half] for half in range(halves)], axis=1).astype(BF))


def fused_kernel(
    rows_dev, cols_dev, classes, factor,
    x_ref, wqkv, wout, wup, wdown, gains,
    o_ref, o_qkv, o_out, o_up, o_down, o_gain, *scratch,
):
    arrived, finished, in_send, in_recv, out_send, out_recv = scratch[:6]
    sums, work, reduce_work = scratch[6:11], scratch[11:16], scratch[16:]
    chunks, peers, _, piece, channels = x_ref.shape
    rows = peers * piece
    mesh_id = pl.DeviceIdType.MESH
    ha, wa = lax.axis_index("ha"), lax.axis_index("wa")
    kind = ha % classes
    me = ha // classes * cols_dev + wa

    def device_of(i):
        e = lax.rem(me + i, peers)
        return e, (e // cols_dev * classes + kind, lax.rem(e, cols_dev))

    barrier = pltpu.get_barrier_semaphore()

    @pl.loop(1, peers)
    def _(i):
        pl.semaphore_signal(barrier, inc=1, device_id=device_of(i)[1], device_id_type=mesh_id)

    extra = classes.bit_length() - 1
    for b in range(extra):
        other = ha + (1 - 2 * ((ha // (1 << b)) % 2)) * (1 << b)
        pl.semaphore_signal(barrier, inc=1, device_id=(other, wa), device_id_type=mesh_id)
    pl.semaphore_wait(barrier, peers - 1 + extra)

    def scatter(src, dst, c, send_sem, recv_sem):
        pltpu.make_async_copy(src.at[c, me], dst.at[c, me], recv_sem.at[c]).start()

        @pl.loop(1, peers)
        def _(i):
            e, device = device_of(i)
            pltpu.make_async_remote_copy(
                src_ref=src.at[c, e], dst_ref=dst.at[c, me],
                send_sem=send_sem.at[c], recv_sem=recv_sem.at[c],
                device_id=device, device_id_type=mesh_id,
            ).start()

    def all_of(ref, c, sem):
        pltpu.make_async_copy(ref.at[c], ref.at[c], sem.at[c]).wait()

    def all_sent(ref, c, sem):
        part = ref.at[c, pl.ds(0, peers - 1)]
        pltpu.make_async_copy(part, part, sem.at[c]).wait()

    @pl.loop(0, chunks)
    def _(c):
        scatter(x_ref, arrived, c, in_send, in_recv)

    for ref in sums:
        ref[...] = jnp.zeros_like(ref)

    @pl.loop(0, chunks)
    def _(c):
        all_of(arrived, c, in_recv)

        def store(value):
            finished[c] = value.reshape(peers, piece, channels)

        chunk_work(
            lambda: arrived[c, :, 0].reshape(rows, channels),
            lambda: arrived[c, :, 1].reshape(rows, channels),
            store, None, wqkv, wout, wup, wdown, gains, *sums, *work,
        )
        scatter(finished, o_ref, c, out_send, out_recv)

    reduce_steps(
        rows_dev, cols_dev, factor, *sums, o_qkv, o_out, o_up, o_down, o_gain, *reduce_work
    )

    @pl.loop(0, chunks)
    def _(c):
        all_of(o_ref, c, out_recv)
        all_sent(finished, c, out_send)
        all_sent(x_ref, c, in_send)


def scratch_of(rows, channels):
    members = GRID * GRID
    halves = channels // LANES
    wide = (HEADS // halves) * members
    return [
        pltpu.VMEM((halves, rows, LANES), F32),
        pltpu.VMEM((rows, 3 * channels), BF),
        pltpu.VMEM((rows // members, halves, members, wide), F32),
        pltpu.VMEM((rows, channels), BF),
        pltpu.VMEM((rows, 3 * channels), BF),
    ]


def reduce_steps(
    rows_dev, cols_dev, factor,
    s_qkv, s_out, s_up, s_down, s_gain,
    o_qkv, o_out, o_up, o_down, o_gain,
    work, send, recv, total, gsend, grecv, gwide, send_sem, recv_sem,
):
    mesh_id = pl.DeviceIdType.MESH
    bits = rows_dev.bit_length() - 1
    half_rows = work.shape[1]
    ha, wa = lax.axis_index("ha"), lax.axis_index("wa")
    side = [(ha // (1 << b)) % 2 for b in range(bits)]
    partner = [(ha + (1 - 2 * side[b]) * (1 << b), wa) for b in range(bits)]
    across = [(ha, lax.rem(wa + i, cols_dev)) for i in range(1, cols_dev)]

    count = [0]
    copies = []

    def push(src, dst, device):
        k = count[0]
        count[0] += 1
        copy = pltpu.make_async_remote_copy(
            src_ref=src, dst_ref=dst, send_sem=send_sem.at[k], recv_sem=recv_sem.at[k],
            device_id=device, device_id_type=mesh_id,
        )
        copy.start()
        copies.append(copy)
        return copy

    places = []
    block = s_qkv.shape[0]
    per_half = half_rows // block
    for src, dst, flip in ((s_qkv, o_qkv, 0), (s_out, o_out, 0), (s_up, o_up, 0), (s_down, o_down, 1)):
        for start in range(0, src.shape[1], LANES):
            places.append((src, dst, flip, start))
    used = -(-len(places) // 2)
    for n, (src, _, _, start) in enumerate(places):
        row = n % used * block
        work[n // used, row : row + block, :] = src[:, start : start + LANES]
    if used < per_half:
        work[:, used * block :, :] = jnp.zeros((2, half_rows - used * block, LANES), F32)

    def span(start, size):
        return pl.ds(pl.multiple_of(start, ROWS), size)

    orders = [[0] + list(range(1, bits)), [0] + list(range(bits - 1, 0, -1))]
    start = [0, 0]
    size = half_rows
    offset = 0
    pending = [None, None]
    gsend[0] = jnp.zeros(gsend.shape[1:], F32)
    gsend[0, 0:2, :] = s_gain[...]
    gpending = None

    def absorb(h):
        if pending[h] is None:
            return
        copy, at, n = pending[h]
        copy.wait_recv()
        place = span(start[h], n)
        work[h, place, :] = work[h, place, :] + recv[h, at : at + n, :].astype(F32)

    for step in range(bits):
        half = size // 2
        for h in range(2):
            absorb(h)
            b = orders[h][step]
            send[h, offset : offset + half, :] = work[h, span(start[h] + (1 - side[b]) * half, half), :].astype(BF)
            copy = push(
                send.at[h, pl.ds(offset, half), :], recv.at[h, pl.ds(offset, half), :], partner[b]
            )
            start[h] = start[h] + side[b] * half
            pending[h] = (copy, offset, half)
        if step > 0:
            gpending.wait_recv()
            gsend[step] = gsend[step - 1] + grecv[step - 1]
        gpending = push(gsend.at[step], grecv.at[step], partner[step])
        offset += half
        size = half

    shard = size // cols_dev
    arrivals = [[], []]
    for h in range(2):
        absorb(h)
        for i in range(1, cols_dev):
            peer = across[i - 1]
            at = offset + (i - 1) * shard
            send[h, at : at + shard, :] = work[h, span(start[h] + peer[1] * shard, shard), :].astype(BF)
            arrivals[h].append(
                push(send.at[h, pl.ds(at, shard), :], recv.at[h, pl.ds(at, shard), :], peer)
            )
    gpending.wait_recv()
    gwide[wa] = gsend[bits - 1] + grecv[bits - 1]
    garrivals = [push(gwide.at[wa], gwide.at[wa], peer) for peer in across]

    gathers = [[], []]
    for h in range(2):
        mine = span(start[h] + wa * shard, shard)
        value = work[h, mine, :]
        for i in range(1, cols_dev):
            arrivals[h][i - 1].wait_recv()
            at = offset + (i - 1) * shard
            value = value + recv[h, at : at + shard, :].astype(F32)
        total[h, mine, :] = value.astype(BF)
        for peer in across:
            gathers[h].append(push(total.at[h, mine, :], total.at[h, mine, :], peer))
    for step in reversed(range(bits)):
        for h in range(2):
            for copy in gathers[h]:
                copy.wait_recv()
            b = orders[h][step]
            held = total.at[h, span(start[h], size), :]
            gathers[h] = [push(held, held, partner[b])]
            start[h] = start[h] - side[b] * size
        size = size * 2
    for copy in garrivals:
        copy.wait_recv()
    gain = gwide[0]
    for i in range(1, cols_dev):
        gain = gain + gwide[i]
    o_gain[...] = gain[0:2, :] * factor
    for h in range(2):
        for copy in gathers[h]:
            copy.wait_recv()
    for n, (_, dst, flip, at) in enumerate(places):
        row = n % used * block
        value = total[n // used, row : row + block, :].astype(F32) * factor
        if flip:
            dst[at : at + LANES, :] = value.T
        else:
            dst[:, at : at + LANES] = value
    for copy in copies:
        copy.wait_send()


def reduce_scratch(rows_dev, cols_dev, elements, channels):
    bits = rows_dev.bit_length() - 1
    unit = ROWS * rows_dev * cols_dev
    half_rows = -(-elements // (2 * LANES * unit)) * unit
    moved = half_rows - half_rows // rows_dev + half_rows // rows_dev // cols_dev * (cols_dev - 1)
    number = 5 * (cols_dev - 1) + 5 * bits
    return [
        pltpu.VMEM((2, half_rows, LANES), F32),
        pltpu.VMEM((2, moved, LANES), BF),
        pltpu.VMEM((2, moved, LANES), BF),
        pltpu.VMEM((2, half_rows, LANES), BF),
        pltpu.VMEM((bits, 8, channels), F32),
        pltpu.VMEM((bits, 8, channels), F32),
        pltpu.VMEM((cols_dev, 8, channels), F32),
        pltpu.SemaphoreType.DMA((number,)),
        pltpu.SemaphoreType.DMA((number,)),
    ]


def fused_call(rows_dev, cols_dev, classes, factor, x, *weights):
    chunks, peers, _, piece, channels = x.shape
    hidden = weights[2].shape[1]
    shapes = [(channels, 3 * channels), (channels, channels), (channels, hidden), (hidden, channels), (2, channels)]
    held = shapes[:3] + [(channels, hidden), (2, channels)]
    elements = sum(math.prod(s) for s in shapes[:4])
    vmem = pl.BlockSpec(memory_space=pltpu.VMEM)
    anywhere = pl.BlockSpec(memory_space=pl.ANY)
    return pl.pallas_call(
        functools.partial(fused_kernel, rows_dev, cols_dev, classes, factor),
        in_specs=[anywhere] + [vmem] * 5,
        out_specs=[anywhere] + [vmem] * 5,
        out_shape=[jax.ShapeDtypeStruct((chunks, peers, piece, channels), BF)]
        + [jax.ShapeDtypeStruct(s, F32) for s in shapes],
        scratch_shapes=[
            pltpu.VMEM((chunks, peers, 2, piece, channels), BF),
            pltpu.VMEM((chunks, peers, piece, channels), BF),
        ]
        + [pltpu.SemaphoreType.DMA((chunks,))] * 4
        + [pltpu.VMEM(s, F32) for s in held]
        + scratch_of(peers * piece, channels)
        + reduce_scratch(rows_dev, cols_dev, elements, channels),
        compiler_params=pltpu.CompilerParams(
            collective_id=0, has_side_effects=True, vmem_limit_bytes=56 << 20
        ),
    )(x, *weights)


def layout(rows_dev, cols_dev, tile_rows, tile_cols):
    stride_h = tile_rows * rows_dev // GRID
    stride_w = tile_cols * cols_dev // GRID
    classes = max(1, stride_h // tile_rows)
    assert stride_h == classes * tile_rows and tile_cols % stride_w == 0
    inner = tile_cols // stride_w
    peers = rows_dev // classes * cols_dev
    mine = tile_rows * stride_w // peers
    assert tile_rows * stride_w == mine * peers and stride_w % mine == 0
    per_chunk = ROWS // inner
    assert mine % per_chunk == 0
    return classes, inner, peers, stride_w // mine, mine // per_chunk, per_chunk


def shards(mesh_shape, features, cotangent, qkv_weight, out_weight, up_weight, down_weight, norm_gains):
    images, tile_rows, tile_cols, channels = features.shape
    rows_dev, cols_dev = mesh_shape["ha"], mesh_shape["wa"]
    classes, inner, peers, cuts, chunks, per_chunk = layout(rows_dev, cols_dev, tile_rows, tile_cols)
    split = (tile_rows, inner, cuts, chunks, per_chunk, channels)

    def pack(tile):
        cut = jnp.transpose(tile.reshape(split), (3, 0, 2, 1, 4, 5))
        return cut.reshape(chunks, peers, ROWS, channels)

    def unpack(packed):
        cut = packed.reshape(chunks, tile_rows, cuts, inner, per_chunk, channels)
        return jnp.transpose(cut, (1, 3, 2, 0, 4, 5)).reshape(images, tile_rows, tile_cols, channels)

    packed = jnp.stack([pack(features), pack(cotangent)], axis=2)
    factor = 1.0 / float(images * tile_rows * tile_cols * rows_dev * cols_dev) ** 0.5
    done, *totals = fused_call(
        rows_dev, cols_dev, classes, factor, packed,
        qkv_weight, out_weight, up_weight, down_weight, norm_gains,
    )
    return (unpack(done), *totals)


def solution(mesh):
    return jax.shard_map(
        functools.partial(shards, dict(mesh.shape)),
        mesh=mesh,
        in_specs=(P(None, "ha", "wa", None), P(None, "ha", "wa", None), P(), P(), P(), P(), P()),
        out_specs=(P(None, "ha", "wa", None), P(), P(), P(), P(), P()),
        check_vma=False,
    )
```

```python
import functools
import math

import jax
import jax.numpy as jnp
from jax import lax
from jax.experimental import pallas as pl
from jax.experimental.pallas import tpu as pltpu
from jax.sharding import PartitionSpec as P

HEADS = 8
GRID = 8
EPS = 1e-05
LANES = 128
ROWS = 16
BF = jnp.bfloat16
F32 = jnp.float32


def mm(a, b, ca=1, cb=0):
    return lax.dot_general(a, b, (((ca,), (cb,)), ((), ())), preferred_element_type=F32)


def norm_forward(values, gain):
    centre = values - jnp.mean(values, axis=-1, keepdims=True)
    scaled = lax.rsqrt(jnp.mean(centre * centre, axis=-1, keepdims=True) + EPS)
    return centre * scaled, scaled


def norm_backward(grad, normed, scaled, gain):
    inner = grad * gain
    first = jnp.mean(inner, axis=-1, keepdims=True)
    second = jnp.mean(inner * normed, axis=-1, keepdims=True)
    return scaled * (inner - first - normed * second)


def head_masks(members, head_dim):
    lane = lax.broadcasted_iota(jnp.int32, (members, LANES), 1) // head_dim
    return [lane == h for h in range(LANES // head_dim)]


def spread(part, masks):
    zero = jnp.zeros_like(part)
    return jnp.concatenate([jnp.where(m, part, zero) for m in masks], axis=0)


def collect(blocks, masks, members):
    out = blocks[:members]
    for h in range(1, len(masks)):
        out = jnp.where(masks[h], blocks[h * members : (h + 1) * members], out)
    return out


def chunk_work(
    load_in, load_cot, store_out, first,
    wqkv, wout, wup, wdown, gains,
    a_qkv, a_out, a_up, a_down, a_gains,
    reg, qkv, probs, mid, rows_out,
):
    rows, channels = mid.shape
    members = GRID * GRID
    head_dim = channels // HEADS
    groups = rows // members
    halves = channels // LANES
    scale = head_dim ** (-0.5)
    masks = head_masks(members, head_dim)
    per_half = len(masks)
    wide = per_half * members

    def add_to(ref, index, value):
        ref[index] = ref[index] + value

    def grouped(load):
        flat = load().astype(F32)
        for half in range(halves):
            reg[half] = flat[:, half * LANES : (half + 1) * LANES]
        return jnp.concatenate(
            [
                jnp.concatenate(
                    [reg[half, pl.ds(j, members, stride=groups), :] for half in range(halves)],
                    axis=1,
                )
                for j in range(groups)
            ],
            axis=0,
        )

    gain_a, gain_b = gains[0:1, :], gains[1:2, :]
    cot = grouped(load_cot)
    cot_low = cot.astype(BF)
    values = grouped(load_in)
    normed_a, scaled_a = norm_forward(values, gain_a)
    input_norm = (normed_a * gain_a).astype(BF)
    qkv[...] = mm(input_norm, wqkv[...]).astype(BF)

    def section(g, which, half):
        start = which * channels + half * LANES
        return qkv[g * members : (g + 1) * members, start : start + LANES]

    for g in range(groups):
        for half in range(halves):
            q, k, v = (section(g, which, half) for which in range(3))
            e = jnp.exp(mm(k, spread(q, masks), 1, 1) * scale)
            p = e / jnp.sum(e, axis=0, keepdims=True)
            probs[g, half] = p
            ctx = collect(mm(p.astype(BF), v, 0, 0), masks, members)
            mid[g * members : (g + 1) * members, half * LANES : (half + 1) * LANES] = ctx.astype(BF)

    context = mid[...]
    hidden = (values + mm(context, wout[...])).astype(BF).astype(F32)
    normed_b, scaled_b = norm_forward(hidden, gain_b)
    mid_norm = (normed_b * gain_b).astype(BF)
    root = math.sqrt(2.0 / math.pi)
    grad_mid = None
    width = 256
    for start in range(0, wup.shape[1], width):
        cols = slice(start, start + width)
        pre = mm(mid_norm, wup[:, cols])
        square = pre * pre
        t = jnp.tanh(root * (pre + 0.044715 * (square * pre)))
        half_up = 0.5 * (1.0 + t)
        act = (pre * half_up).astype(BF)
        slope = half_up + (0.5 * root) * pre * (1.0 - t * t) * (1.0 + (3 * 0.044715) * square)
        grad_pre = (mm(cot_low, wdown[cols, :], 1, 1) * slope).astype(BF)
        add_to(a_down, (slice(None), cols), mm(cot_low, act, 0, 0))
        add_to(a_up, (slice(None), cols), mm(mid_norm, grad_pre, 0, 0))
        part = mm(grad_pre, wup[:, cols], 1, 1)
        grad_mid = part if grad_mid is None else grad_mid + part
    add_to(a_gains, (slice(1, 2), slice(None)), jnp.sum(grad_mid * normed_b, axis=0, keepdims=True))
    grad_hidden = (cot + norm_backward(grad_mid, normed_b, scaled_b, gain_b)).astype(BF)
    add_to(a_out, Ellipsis, mm(context, grad_hidden, 0, 0))
    mid[...] = mm(grad_hidden, wout[...], 1, 1).astype(BF)

    for g in range(groups):
        at = slice(g * members, (g + 1) * members)
        for half in range(halves):
            q, k, v = (section(g, which, half) for which in range(3))
            p = probs[g, half]
            gc = spread(mid[at, half * LANES : (half + 1) * LANES], masks)
            gp = mm(v, gc, 1, 1)
            gs = (p * (gp - jnp.sum(p * gp, axis=0, keepdims=True)) * scale).astype(BF)
            grads = (
                collect(mm(gs, k, 0, 0), masks, members),
                mm(gs, spread(q, masks)),
                mm(p.astype(BF), gc),
            )
            for which in range(3):
                begin = which * channels + half * LANES
                rows_out[at, begin : begin + LANES] = grads[which].astype(BF)

    grad_rows = rows_out[...]
    add_to(a_qkv, Ellipsis, mm(input_norm, grad_rows, 0, 0))
    grad_norm = mm(grad_rows, wqkv[...], 1, 1)
    add_to(a_gains, (slice(0, 1), slice(None)), jnp.sum(grad_norm * normed_a, axis=0, keepdims=True))
    result = grad_hidden.astype(F32) + norm_backward(grad_norm, normed_a, scaled_a, gain_a)
    for half in range(halves):
        for j in range(groups):
            reg[half, pl.ds(j, members, stride=groups), :] = result[
                j * members : (j + 1) * members, half * LANES : (half + 1) * LANES
            ]
    store_out(jnp.concatenate([reg[half] for half in range(halves)], axis=1).astype(BF))


def fused_kernel(
    rows_dev, cols_dev, classes, factor,
    x_ref, wqkv, wout, wup, wdown, gains,
    o_ref, o_qkv, o_out, o_up, o_down, o_gain, *scratch,
):
    arrived, finished, in_send, in_recv, out_send, out_recv = scratch[:6]
    sums, work, reduce_work = scratch[6:11], scratch[11:16], scratch[16:]
    chunks, peers, _, piece, channels = x_ref.shape
    rows = peers * piece
    mesh_id = pl.DeviceIdType.MESH
    ha, wa = lax.axis_index("ha"), lax.axis_index("wa")
    kind = ha % classes
    me = ha // classes * cols_dev + wa

    def device_of(i):
        tall = peers // cols_dev
        e = lax.rem(me // cols_dev + lax.rem(i, tall), tall) * cols_dev + lax.rem(wa + i // tall, cols_dev)
        return e, (e // cols_dev * classes + kind, lax.rem(e, cols_dev))

    barrier = pltpu.get_barrier_semaphore()

    @pl.loop(1, peers)
    def _(i):
        pl.semaphore_signal(barrier, inc=1, device_id=device_of(i)[1], device_id_type=mesh_id)

    extra = classes.bit_length() - 1
    for b in range(extra):
        other = ha + (1 - 2 * ((ha // (1 << b)) % 2)) * (1 << b)
        pl.semaphore_signal(barrier, inc=1, device_id=(other, wa), device_id_type=mesh_id)
    pl.semaphore_wait(barrier, peers - 1 + extra)

    def scatter(src, dst, c, send_sem, recv_sem):
        pltpu.make_async_copy(src.at[c, me], dst.at[c, me], recv_sem.at[c]).start()

        @pl.loop(1, peers)
        def _(i):
            e, device = device_of(i)
            pltpu.make_async_remote_copy(
                src_ref=src.at[c, e], dst_ref=dst.at[c, me],
                send_sem=send_sem.at[c], recv_sem=recv_sem.at[c],
                device_id=device, device_id_type=mesh_id,
            ).start()

    def all_of(ref, c, sem):
        pltpu.make_async_copy(ref.at[c], ref.at[c], sem.at[c]).wait()

    def all_sent(ref, c, sem):
        part = ref.at[c, pl.ds(0, peers - 1)]
        pltpu.make_async_copy(part, part, sem.at[c]).wait()

    ahead = 2

    @pl.loop(0, ahead)
    def _(c):
        scatter(x_ref, arrived, c, in_send, in_recv)

    for ref in sums:
        ref[...] = jnp.zeros_like(ref)

    @pl.loop(0, chunks)
    def _(c):
        all_of(arrived, c, in_recv)

        @pl.when(c + ahead < chunks)
        def _():
            scatter(x_ref, arrived, c + ahead, in_send, in_recv)

        def store(value):
            finished[c] = value.reshape(peers, piece, channels)

        chunk_work(
            lambda: arrived[c, :, 0].reshape(rows, channels),
            lambda: arrived[c, :, 1].reshape(rows, channels),
            store, None, wqkv, wout, wup, wdown, gains, *sums, *work,
        )
        scatter(finished, o_ref, c, out_send, out_recv)

    reduce_steps(
        rows_dev, cols_dev, factor, *sums, o_qkv, o_out, o_up, o_down, o_gain, *reduce_work
    )

    @pl.loop(0, chunks)
    def _(c):
        all_of(o_ref, c, out_recv)
        all_sent(finished, c, out_send)
        all_sent(x_ref, c, in_send)


def scratch_of(rows, channels):
    members = GRID * GRID
    halves = channels // LANES
    wide = (HEADS // halves) * members
    return [
        pltpu.VMEM((halves, rows, LANES), F32),
        pltpu.VMEM((rows, 3 * channels), BF),
        pltpu.VMEM((rows // members, halves, members, wide), F32),
        pltpu.VMEM((rows, channels), BF),
        pltpu.VMEM((rows, 3 * channels), BF),
    ]


def reduce_steps(
    rows_dev, cols_dev, factor,
    s_qkv, s_out, s_up, s_down, s_gain,
    o_qkv, o_out, o_up, o_down, o_gain,
    work, send, recv, total, gsend, grecv, gwide, send_sem, recv_sem,
):
    mesh_id = pl.DeviceIdType.MESH
    bits = rows_dev.bit_length() - 1
    half_rows = work.shape[1]
    ha, wa = lax.axis_index("ha"), lax.axis_index("wa")
    side = [(ha // (1 << b)) % 2 for b in range(bits)]
    partner = [(ha + (1 - 2 * side[b]) * (1 << b), wa) for b in range(bits)]
    across = [(ha, lax.rem(wa + i, cols_dev)) for i in range(1, cols_dev)]

    count = [0]
    copies = []

    def push(src, dst, device):
        k = count[0]
        count[0] += 1
        copy = pltpu.make_async_remote_copy(
            src_ref=src, dst_ref=dst, send_sem=send_sem.at[k], recv_sem=recv_sem.at[k],
            device_id=device, device_id_type=mesh_id,
        )
        copy.start()
        copies.append(copy)
        return copy

    places = []
    block = s_qkv.shape[0]
    per_half = half_rows // block
    for src, dst, flip in ((s_qkv, o_qkv, 0), (s_out, o_out, 0), (s_up, o_up, 0), (s_down, o_down, 1)):
        for start in range(0, src.shape[1], LANES):
            places.append((src, dst, flip, start))
    used = -(-len(places) // 2)
    for n, (src, _, _, start) in enumerate(places):
        row = n % used * block
        work[n // used, row : row + block, :] = src[:, start : start + LANES]
    if used < per_half:
        work[:, used * block :, :] = jnp.zeros((2, half_rows - used * block, LANES), F32)

    def span(start, size):
        return pl.ds(pl.multiple_of(start, ROWS), size)

    orders = [[0] + list(range(1, bits)), [0] + list(range(bits - 1, 0, -1))]
    start = [0, 0]
    size = half_rows
    offset = 0
    pending = [None, None]
    gsend[0] = jnp.zeros(gsend.shape[1:], F32)
    gsend[0, 0:2, :] = s_gain[...]
    gpending = None

    def absorb(h):
        if pending[h] is None:
            return
        copy, at, n = pending[h]
        copy.wait_recv()
        place = span(start[h], n)
        work[h, place, :] = work[h, place, :] + recv[h, at : at + n, :].astype(F32)

    for step in range(bits):
        half = size // 2
        for h in range(2):
            absorb(h)
            b = orders[h][step]
            send[h, offset : offset + half, :] = work[h, span(start[h] + (1 - side[b]) * half, half), :].astype(BF)
            copy = push(
                send.at[h, pl.ds(offset, half), :], recv.at[h, pl.ds(offset, half), :], partner[b]
            )
            start[h] = start[h] + side[b] * half
            pending[h] = (copy, offset, half)
        if step > 0:
            gpending.wait_recv()
            gsend[step] = gsend[step - 1] + grecv[step - 1]
        gpending = push(gsend.at[step], grecv.at[step], partner[step])
        offset += half
        size = half

    shard = size // cols_dev
    arrivals = [[], []]
    for h in range(2):
        absorb(h)
        for i in range(1, cols_dev):
            peer = across[i - 1]
            at = offset + (i - 1) * shard
            send[h, at : at + shard, :] = work[h, span(start[h] + peer[1] * shard, shard), :].astype(BF)
            arrivals[h].append(
                push(send.at[h, pl.ds(at, shard), :], recv.at[h, pl.ds(at, shard), :], peer)
            )
    gpending.wait_recv()
    gwide[wa] = gsend[bits - 1] + grecv[bits - 1]
    garrivals = [push(gwide.at[wa], gwide.at[wa], peer) for peer in across]

    gathers = [[], []]
    for h in range(2):
        mine = span(start[h] + wa * shard, shard)
        value = work[h, mine, :]
        for i in range(1, cols_dev):
            arrivals[h][i - 1].wait_recv()
            at = offset + (i - 1) * shard
            value = value + recv[h, at : at + shard, :].astype(F32)
        total[h, mine, :] = value.astype(BF)
        for peer in across:
            gathers[h].append(push(total.at[h, mine, :], total.at[h, mine, :], peer))
    for step in reversed(range(bits)):
        for h in range(2):
            for copy in gathers[h]:
                copy.wait_recv()
            b = orders[h][step]
            held = total.at[h, span(start[h], size), :]
            gathers[h] = [push(held, held, partner[b])]
            start[h] = start[h] - side[b] * size
        size = size * 2
    for copy in garrivals:
        copy.wait_recv()
    gain = gwide[0]
    for i in range(1, cols_dev):
        gain = gain + gwide[i]
    o_gain[...] = gain[0:2, :] * factor
    for h in range(2):
        for copy in gathers[h]:
            copy.wait_recv()
    for n, (_, dst, flip, at) in enumerate(places):
        row = n % used * block
        value = total[n // used, row : row + block, :].astype(F32) * factor
        if flip:
            dst[at : at + LANES, :] = value.T
        else:
            dst[:, at : at + LANES] = value
    for copy in copies:
        copy.wait_send()


def reduce_scratch(rows_dev, cols_dev, elements, channels):
    bits = rows_dev.bit_length() - 1
    unit = ROWS * rows_dev * cols_dev
    half_rows = -(-elements // (2 * LANES * unit)) * unit
    moved = half_rows - half_rows // rows_dev + half_rows // rows_dev // cols_dev * (cols_dev - 1)
    number = 5 * (cols_dev - 1) + 5 * bits
    return [
        pltpu.VMEM((2, half_rows, LANES), F32),
        pltpu.VMEM((2, moved, LANES), BF),
        pltpu.VMEM((2, moved, LANES), BF),
        pltpu.VMEM((2, half_rows, LANES), BF),
        pltpu.VMEM((bits, 8, channels), F32),
        pltpu.VMEM((bits, 8, channels), F32),
        pltpu.VMEM((cols_dev, 8, channels), F32),
        pltpu.SemaphoreType.DMA((number,)),
        pltpu.SemaphoreType.DMA((number,)),
    ]


def fused_call(rows_dev, cols_dev, classes, factor, x, *weights):
    chunks, peers, _, piece, channels = x.shape
    hidden = weights[2].shape[1]
    shapes = [(channels, 3 * channels), (channels, channels), (channels, hidden), (hidden, channels), (2, channels)]
    held = shapes[:3] + [(channels, hidden), (2, channels)]
    elements = sum(math.prod(s) for s in shapes[:4])
    vmem = pl.BlockSpec(memory_space=pltpu.VMEM)
    anywhere = pl.BlockSpec(memory_space=pl.ANY)
    return pl.pallas_call(
        functools.partial(fused_kernel, rows_dev, cols_dev, classes, factor),
        in_specs=[anywhere] + [vmem] * 5,
        out_specs=[anywhere] + [vmem] * 5,
        out_shape=[jax.ShapeDtypeStruct((chunks, peers, piece, channels), BF)]
        + [jax.ShapeDtypeStruct(s, F32) for s in shapes],
        scratch_shapes=[
            pltpu.VMEM((chunks, peers, 2, piece, channels), BF),
            pltpu.VMEM((chunks, peers, piece, channels), BF),
        ]
        + [pltpu.SemaphoreType.DMA((chunks,))] * 4
        + [pltpu.VMEM(s, F32) for s in held]
        + scratch_of(peers * piece, channels)
        + reduce_scratch(rows_dev, cols_dev, elements, channels),
        compiler_params=pltpu.CompilerParams(
            collective_id=0, has_side_effects=True, vmem_limit_bytes=56 << 20
        ),
    )(x, *weights)


def layout(rows_dev, cols_dev, tile_rows, tile_cols):
    stride_h = tile_rows * rows_dev // GRID
    stride_w = tile_cols * cols_dev // GRID
    classes = max(1, stride_h // tile_rows)
    assert stride_h == classes * tile_rows and tile_cols % stride_w == 0
    inner = tile_cols // stride_w
    peers = rows_dev // classes * cols_dev
    mine = tile_rows * stride_w // peers
    assert tile_rows * stride_w == mine * peers and stride_w % mine == 0
    per_chunk = ROWS // inner
    assert mine % per_chunk == 0
    return classes, inner, peers, stride_w // mine, mine // per_chunk, per_chunk


def shards(mesh_shape, features, cotangent, qkv_weight, out_weight, up_weight, down_weight, norm_gains):
    images, tile_rows, tile_cols, channels = features.shape
    rows_dev, cols_dev = mesh_shape["ha"], mesh_shape["wa"]
    classes, inner, peers, cuts, chunks, per_chunk = layout(rows_dev, cols_dev, tile_rows, tile_cols)
    split = (tile_rows, inner, cuts, chunks, per_chunk, channels)

    def pack(tile):
        cut = jnp.transpose(tile.reshape(split), (3, 0, 2, 1, 4, 5))
        return cut.reshape(chunks, peers, ROWS, channels)

    def unpack(packed):
        cut = packed.reshape(chunks, tile_rows, cuts, inner, per_chunk, channels)
        return jnp.transpose(cut, (1, 3, 2, 0, 4, 5)).reshape(images, tile_rows, tile_cols, channels)

    packed = jnp.stack([pack(features), pack(cotangent)], axis=2)
    factor = 1.0 / float(images * tile_rows * tile_cols * rows_dev * cols_dev) ** 0.5
    done, *totals = fused_call(
        rows_dev, cols_dev, classes, factor, packed,
        qkv_weight, out_weight, up_weight, down_weight, norm_gains,
    )
    return (unpack(done), *totals)


def solution(mesh):
    return jax.shard_map(
        functools.partial(shards, dict(mesh.shape)),
        mesh=mesh,
        in_specs=(P(None, "ha", "wa", None), P(None, "ha", "wa", None), P(), P(), P(), P(), P()),
        out_specs=(P(None, "ha", "wa", None), P(), P(), P(), P(), P()),
        check_vma=False,
    )
```
